32 devices in a mesh: scene: 2 (over x), gx: 16 (over z, y, core).
Axes of the slice: x: 2, y: 2, z: 4, core: 2. Of those that a mesh axis runs over, the one named last changes fastest.
Arguments:
- feats: bfloat16 [128, 64, 256], P(('scene', 'gx')), parts along dimension 0, may hold values from -6 to 6
- voxel_mask: int32 [128, 64], P(('scene', 'gx')), parts along dimension 0, may hold values 0 or 1
- brick_table: int32 [128, 27], P(('scene', 'gx')), parts along dimension 0, may hold values from 0 to 12, as said below
- counts: int32 [32], P(('scene', 'gx')), parts along dimension 0, may hold values from 1 to 4, as said below
- weight_one: bfloat16 [6912, 256], replicated, may hold values from -0.078125 to 0.078125
- weight_two: bfloat16 [6912, 256], replicated, may hold values from -0.078125 to 0.078125
- cotangent: bfloat16 [128, 64, 256], P(('scene', 'gx')), parts along dimension 0, may hold values from -6 to 6
Outputs:
- block_out: bfloat16 [128, 64, 256], P(('scene', 'gx')), parts along dimension 0
- feats_grad: bfloat16 [128, 64, 256], P(('scene', 'gx')), parts along dimension 0
- grad_one: float32 [13824, 256], P(('scene', 'gx')), parts along dimension 0
The draws below stay inside these ranges and needn't reach their ends.
There are 2 independent parts, one for each index of `scene`. The reference program is written for one: setup_inputs(seed, part) draws one part's arguments, and reference() takes and returns one part's arrays. A program takes and returns all parts, laid end to end along the dimension named above; an argument that names none is the same for every part. Nothing has to cross between parts.
Inputs may be any that keep to these rules, and one draw needn't show every extreme that they name: `counts`: every owner has between 4 // 4 (at least 1) and 4 active bricks; both ends are taken by some owner in every draw. `brick_table`: entry q = 9 (dx + 1) + 3 (dy + 1) + (dz + 1). Values below 4 (the left owner's slots) appear only where dx = -1 and values from 8 to 3 * 4 - 1 (the right owner's) only where dx = +1; they name only active slots, and the first owner never names a left slot, the last never a right one. Entry 13 of an active slot is 4 plus the slot itself; 12 means no neighbour; inactive slots hold 12 everywhere and are never named.
All inputs are finite; a program needn't handle non-finite values. No bound on the sum of `voxel_mask` on one device may be relied on, other than what follows from the above.
Results may differ from the reference program's by a relative error of at most 0.0029.
Values may be sent and summed in bfloat16 or wider, within the bound.
A program may use at most 128 MiB of HBM per device.

```python
import jax
import jax.numpy as jnp
import numpy as np
from jax import lax

C = 256
VB = 64
BR = 4
BRICKS = 64
KC = 6912
N_GX = 16


def shared_layout(key):
    count_key, pick_key, empty_key, side_key, end_key, low_key = jax.random.split(key, 6)
    lowest = max(BR // 4, 1)
    counts = jax.random.randint(count_key, (N_GX,), lowest, BR + 1)
    full = jax.random.randint(end_key, (), 0, N_GX)
    least = (full + 1 + jax.random.randint(low_key, (), 0, N_GX - 1)) % N_GX
    owners = jnp.arange(N_GX)
    counts = jnp.where(owners == least, lowest, counts)
    counts = jnp.where(owners == full, BR, counts).astype(jnp.int32)
    owner = jnp.arange(BRICKS) // BR
    slot = jnp.arange(BRICKS) % BR
    step_x = jnp.asarray(np.arange(27) // 9 - 1)[None, :]
    pick = jax.random.randint(pick_key, (BRICKS, 27), 0, 2 ** 20)
    side = jax.random.randint(side_key, (BRICKS, 27), 0, 2)
    empty = jax.random.randint(empty_key, (BRICKS, 27), 0, 10) < 3
    own_count = counts[owner][:, None]
    left_count = counts[jnp.clip(owner - 1, 0, N_GX - 1)][:, None]
    right_count = counts[jnp.clip(owner + 1, 0, N_GX - 1)][:, None]
    use_left = (step_x == -1) & (side == 1) & (owner[:, None] > 0)
    use_right = (step_x == 1) & (side == 1) & (owner[:, None] < N_GX - 1)
    entry = jnp.where(use_left, pick % left_count, jnp.where(use_right, 2 * BR + pick % right_count, BR + pick % own_count))
    entry = jnp.where(empty, 3 * BR, entry)
    centre = jnp.arange(27)[None, :] == 13
    entry = jnp.where(centre, BR + slot[:, None], entry)
    entry = jnp.where(slot[:, None] >= own_count, 3 * BR, entry)
    return (counts, entry.astype(jnp.int32))


def draw_brick_table(key, part):
    counts, entry = shared_layout(key)
    return entry


def draw_counts(key, part):
    counts, entry = shared_layout(key)
    return counts


def place_ends(entries, stream_key, smallest, high):
    index_at = [jax.random.randint(jax.random.fold_in(stream_key, axis), (), 0, length) for axis, length in enumerate(entries.shape)]
    longest = entries.shape.index(max(entries.shape))
    next_to = index_at[:longest] + [(index_at[longest] + 1) % entries.shape[longest]] + index_at[longest + 1:]
    return entries.at[tuple(index_at)].set(smallest).at[tuple(next_to)].set(high)


def strengthened(result, rng, source, target, blocks, factor):
    owner, partner = [(jnp.arange(result.shape[axis_at]) // (result.shape[axis_at] // blocks)).reshape([-1 if axis == axis_at else 1 for axis in range(result.ndim)]) for axis_at in (source, target)]
    chosen = jax.random.permutation(rng, blocks)[partner]
    strong = (owner == chosen) | (owner == (partner + blocks // 2) % blocks)
    return jnp.where(strong, factor * result, result)


def levels(key, dims, cuts, low, top_value):
    loudness, own = 1.0, jax.random.fold_in(key, 6)
    for dim, blocks in cuts:
        steps = jnp.exp(jax.random.uniform(jax.random.fold_in(own, dim), (blocks,), jnp.float32, low / len(cuts), top_value / len(cuts)))
        loudness = loudness * jnp.repeat(steps, dims[dim] // blocks).reshape([-1 if axis == dim else 1 for axis in range(len(dims))])
    return loudness


def centred(rng, dims, spread, most, cuts=(), kind=jnp.bfloat16):
    result = jax.random.normal(rng, dims, jnp.float32) * spread
    if len(cuts) > 0:
        result = levels(rng, dims, cuts, -0.22, 0.18) * result
    return jnp.clip(result, min=-most, max=most).astype(kind)


def noise_with(rng, shape, spread, bound, cuts, heavy, held_as=jnp.bfloat16):
    entries = spread * jax.random.normal(rng, shape, jnp.float32)
    if cuts:
        entries = entries * levels(rng, shape, cuts, -0.22, 0.18)
    return jnp.clip(strengthened(entries, jax.random.fold_in(rng, 3), *heavy), -bound, bound).astype(held_as)


def setup_inputs(seed: int = 0, part: int = 0) -> dict:
    splits = jax.random.split(jax.random.key(seed), 8)
    part_keys = jax.random.split(jax.random.fold_in(splits[7], part), 8)
    feats = centred(part_keys[0], (BRICKS, VB, C), 1.0, 6.0, ((0, 16),))
    voxel_mask = place_ends((jax.random.randint(part_keys[1], (BRICKS, VB), 0, 5) < 3).astype(jnp.int32), jax.random.fold_in(part_keys[1], 1), 0, 1)
    brick_table = draw_brick_table(jax.random.fold_in(jax.random.fold_in(splits[7], part), 71), part)
    counts = draw_counts(jax.random.fold_in(jax.random.fold_in(splits[7], part), 71), part)
    weight_one = centred(splits[4], (KC, C), KC ** -0.5, 0.078125)
    weight_two = centred(splits[5], (KC, C), KC ** -0.5, 0.078125)
    cotangent = noise_with(part_keys[6], (BRICKS, VB, C), 1.0, 6.0, ((0, 16),), (0, 2, 16, 2.0))
    return {"feats": feats, "voxel_mask": voxel_mask, "brick_table": brick_table, "counts": counts, "weight_one": weight_one, "weight_two": weight_two, "cotangent": cotangent}


def offset_tables():
    brick_of = np.zeros((64, 27), np.int32)
    voxel_of = np.zeros((64, 27), np.int32)
    for voxel in range(64):
        pos = (voxel // 16, voxel // 4 % 4, voxel % 4)
        for offset in range(27):
            step = (offset // 9 - 1, offset // 3 % 3 - 1, offset % 3 - 1)
            moved = [pos[n] + step[n] for n in range(3)]
            brick_of[voxel, offset] = sum(((moved[n] // 4 + 1) * (9, 3, 1)[n] for n in range(3)))
            voxel_of[voxel, offset] = sum((moved[n] % 4 * (16, 4, 1)[n] for n in range(3)))
    return (brick_of, voxel_of)

def silu_slope(value):
    sig = jax.nn.sigmoid(value)
    return sig * (1.0 + value * (1.0 - sig))

def reference(feats, voxel_mask, brick_table, counts, weight_one, weight_two, cotangent):
    nbricks, vb, ch = feats.shape
    per = nbricks // N_GX
    owner = (jnp.arange(nbricks) // per).astype(jnp.int32)
    slot = (jnp.arange(nbricks) % per).astype(jnp.int32)
    active = (slot < counts[owner]).astype(jnp.int32)
    mask = (voxel_mask * active[:, None]).astype(jnp.bfloat16)[:, :, None]
    maskf = mask.astype(jnp.float32)
    entry = brick_table
    col = owner[:, None]
    glob = jnp.where(entry < per, (col - 1) * per + entry, jnp.where(entry < 2 * per, col * per + entry - per, jnp.where(entry < 3 * per, (col + 1) * per + entry - 2 * per, nbricks)))
    glob = jnp.clip(glob, 0, nbricks).astype(jnp.int32)
    brick_of, voxel_of = offset_tables()
    rows = glob[:, brick_of] * vb + jnp.asarray(voxel_of)[None]
    rows = rows.reshape(N_GX, per * vb * 27).astype(jnp.int32)

    def flat(field):
        return jnp.concatenate([field.reshape(nbricks * vb, ch), jnp.zeros((vb, ch), field.dtype)], 0)

    def conv(field, weight):
        table = flat(field)
        out = lax.map(lambda r: jnp.dot(table[r].reshape(per * vb, 27 * ch), weight, preferred_element_type=jnp.float32), rows)
        return out.reshape(nbricks, vb, ch)

    def kernel_grad(field, grad):
        table = flat(field)
        gblocks = grad.reshape(N_GX, per * vb, ch)

        def add(total, pair):
            r, g = pair
            return (total + jnp.dot(table[r].reshape(per * vb, 27 * ch).T, g, preferred_element_type=jnp.float32), None)
        total, _ = lax.scan(add, jnp.zeros((27 * ch, ch), jnp.float32), (rows, gblocks))
        return total

    def back(grad, weight):
        gblocks = grad.reshape(N_GX, per * vb, ch)

        def add(total, pair):
            r, g = pair
            part = lax.dot_general(g, weight, (((1,), (1,)), ((), ())), preferred_element_type=jnp.float32)
            return (total.at[r].add(part.reshape(-1, ch)), None)
        total, _ = lax.scan(add, jnp.zeros(((nbricks + 1) * vb, ch), jnp.float32), (rows, gblocks))
        return total[:nbricks * vb].reshape(nbricks, vb, ch)
    x0 = feats * mask
    y1 = maskf * conv(x0, weight_one)
    a1 = jax.nn.silu(y1).astype(jnp.bfloat16)
    y2 = maskf * conv(a1, weight_two)
    block_out = (y2 + x0.astype(jnp.float32)).astype(jnp.bfloat16)
    g2 = cotangent * mask
    da1 = back(g2, weight_two)
    g1 = (maskf * da1 * silu_slope(y1)).astype(jnp.bfloat16)
    grad_one = kernel_grad(x0, g1)
    feats_grad = (maskf * (back(g1, weight_one) + g2.astype(jnp.float32))).astype(jnp.bfloat16)
    return (block_out, feats_grad, grad_one)
```

```python
import jax
import jax.numpy as jnp
from jax import lax
from jax.experimental import pallas as pl
from jax.experimental.pallas import tpu as pltpu
from jax.sharding import PartitionSpec as P

F32, BF16 = jnp.float32, jnp.bfloat16
VMEM = pl.BlockSpec(memory_space=pltpu.VMEM)
SMEM = pl.BlockSpec(memory_space=pltpu.SMEM)

ROWS, SIDE = 256, 16


def iota(shape, dim):
    return lax.broadcasted_iota(jnp.int32, shape, dim)


def natural_of(row):
    return ((row >> 2) & 3) * 64 + (row >> 6) * 16 + ((row >> 4) & 3) * 4 + (row & 3)


def to_rows():
    shape = (ROWS, ROWS)
    return (natural_of(iota(shape, 0)) == iota(shape, 1)).astype(F32).astype(BF16)


def from_rows():
    shape = (ROWS, ROWS)
    return (natural_of(iota(shape, 1)) == iota(shape, 0)).astype(F32).astype(BF16)


def mat(a, b):
    return jnp.dot(a, b, preferred_element_type=F32)


def mask_rows(mask_ref, counts_ref):
    row = iota((ROWS, 64), 0)
    brick = (row >> 2) & 3
    held = mask_ref[...].astype(F32)
    spread = jnp.zeros((ROWS, 64), F32)
    for b in range(4):
        spread = jnp.where(brick == b, held[b : b + 1, :], spread)
    keep = (iota((ROWS, 64), 1) == (natural_of(row) & 63)) & (brick < counts_ref[0])
    return jnp.sum(jnp.where(keep, spread, 0.0), axis=1, keepdims=True)


def pickers(table_ref):
    row = iota((128, 27), 0) & 63
    shift, brick, k = row >> 4, (row >> 2) & 3, row & 3
    moved = k + shift - 1
    step = jnp.where(moved < 0, 0, jnp.where(moved > 3, 2, 1))
    held = table_ref[...].astype(F32)
    spread = jnp.zeros((128, 27), F32)
    for b in range(4):
        spread = jnp.where(brick == b, held[b : b + 1, :], spread)
    lane = iota((128, 128), 1)
    wide = iota((128, 128), 0) & 63
    source = ((wide & 3) + (wide >> 4) - 1) & 3
    fits = ((lane & 3) == source) & (wide < 48)
    picks = {}
    for qa in range(3):
        for qb in range(3):
            chosen = iota((128, 27), 1) == qa * 9 + qb * 3 + step
            entry = jnp.sum(jnp.where(chosen, spread, 0.0), axis=1, keepdims=True)
            hit = fits & (entry.astype(jnp.int32) == (lane >> 2)) & (lane < 48)
            picks[qa, qb] = hit.astype(F32)
    return picks


def places():
    for wi in range(6):
        for wj in range(6):
            qa, qb = (wi + 3) // 4, (wj + 3) // 4
            yield wi, wj, (qa, qb), (wi + 3) % 4, (wj + 3) % 4


def gather_windows(picks, lower, own, upper, win):
    half = {key: value[:48, :48].astype(BF16) for key, value in picks.items()}
    for wi, wj, q, i, j in places():
        at = pl.ds((i * 4 + j) * SIDE, SIDE)
        source = jnp.concatenate([lower[at], own[at], upper[at]], 0)
        got = mat(half[q], source).astype(BF16)
        for c in range(3):
            win[c, wi, wj] = got[c * SIDE : (c + 1) * SIDE]


def build_stack(win, stack):
    for o in range(27):
        a, b, c = o // 9, o // 3 % 3, o % 3
        stack[:, o * 256 : (o + 1) * 256] = win[c, a : a + 4, b : b + 4].reshape(ROWS, 256)


def spread_back(picks, grad, weight_ref, acc, own, lower, upper):
    acc[...] = jnp.zeros(acc.shape, F32)
    for o in range(27):
        a, b, c = o // 9, o // 3 % 3, o % 3
        part = lax.dot_general(
            grad,
            weight_ref[o * 256 : (o + 1) * 256, :],
            (((1,), (1,)), ((), ())),
            preferred_element_type=F32,
        )
        acc[c, a : a + 4, b : b + 4] += part.reshape(4, 4, SIDE, 256)
    turned = {key: value.T[:48].astype(BF16) for key, value in picks.items()}
    pad = jnp.zeros((SIDE, 256), BF16)
    totals = {}
    for wi, wj, q, i, j in places():
        held = acc[:, wi, wj].reshape(48, 256)
        high = held.astype(BF16)
        low = (held - high.astype(F32)).astype(BF16)
        got = mat(turned[q], jnp.concatenate([high, pad, low, pad], 0))
        totals[i, j] = totals[i, j] + got if (i, j) in totals else got
    for (i, j), value in totals.items():
        at = pl.ds((i * 4 + j) * SIDE, SIDE)
        lower[at] = value[:16].astype(BF16)
        own[at] = value[16:32]
        upper[at] = value[32:48].astype(BF16)


def first_kernel(feats, cot, mask, table, counts, w2, x0, g2, own, lower, upper, acc):
    keep = mask_rows(mask, counts)
    turn = to_rows()
    x0[...] = (mat(turn, feats[...]) * keep).astype(BF16)
    grad = (mat(turn, cot[...]) * keep).astype(BF16)
    g2[...] = grad
    spread_back(pickers(table), grad, w2, acc, own, lower, upper)


def second_kernel(
    x0_low, x0, x0_up, d_own, d_up, d_low, mask, table, counts, w1,
    a1, own, lower, upper, grad_w, win, stack, acc,
):
    keep = mask_rows(mask, counts)
    picks = pickers(table)
    gather_windows(picks, x0_low, x0, x0_up, win)
    build_stack(win, stack)
    y1 = mat(stack[...], w1[...]) * keep
    sig = 1.0 / (1.0 + jnp.exp(-y1))
    a1[...] = (y1 * sig).astype(BF16)
    da1 = d_own[...] + d_up[...].astype(F32) + d_low[...].astype(F32)
    g1 = (da1 * keep * (sig * (1.0 + y1 * (1.0 - sig)))).astype(BF16)
    for o in range(27):
        at = slice(o * 256, (o + 1) * 256)
        grad_w[at, :] = lax.dot_general(
            stack[:, at], g1, (((0,), (0,)), ((), ())), preferred_element_type=F32
        )
    spread_back(picks, g1, w1, acc, own, lower, upper)


def third_kernel(
    a_low, a1, a_up, f_own, f_up, f_low, x0, g2, mask, table, counts, w2,
    block_out, feats_grad, win, stack,
):
    keep = mask_rows(mask, counts)
    gather_windows(pickers(table), a_low, a1, a_up, win)
    build_stack(win, stack)
    y2 = mat(stack[...], w2[...]) * keep
    out = (y2 + x0[...].astype(F32)).astype(BF16)
    turn = from_rows()
    block_out[...] = mat(turn, out).astype(BF16)
    total = f_own[...] + f_up[...].astype(F32) + f_low[...].astype(F32)
    grad = (keep * (total + g2[...].astype(F32))).astype(BF16)
    feats_grad[...] = mat(turn, grad).astype(BF16)


def rows_of(kind):
    return jax.ShapeDtypeStruct((ROWS, 256), kind)


PARAMS = pltpu.CompilerParams(vmem_limit_bytes=50 * 2**20)
WIN = pltpu.VMEM((3, 6, 6, SIDE, 256), BF16)
ACC = pltpu.VMEM((3, 6, 6, SIDE, 256), F32)
STACK = pltpu.VMEM((ROWS, 6912), BF16)


def shifted(value, steps):
    count = lax.axis_size("gx")
    first, last = (max(0, -steps), min(count, count - steps))
    return lax.ppermute(value, "gx", [(source, source + steps) for source in range(first, last)])


def exchange(field, lower, upper):
    up = shifted(jnp.concatenate([field, upper], 0), 1)
    down = shifted(jnp.concatenate([field, lower], 0), -1)
    return up[:ROWS], down[:ROWS], up[ROWS:], down[ROWS:]


def on_device(feats, voxel_mask, brick_table, counts, weight_one, weight_two, cotangent):
    per, vb, ch = feats.shape
    kc = weight_one.shape[0]
    small = (voxel_mask, brick_table, counts)
    small_specs = [VMEM, VMEM, SMEM]
    x0, g2, d_own, d_lower, d_upper = pl.pallas_call(
        first_kernel,
        out_shape=[rows_of(BF16), rows_of(BF16), rows_of(F32), rows_of(BF16), rows_of(BF16)],
        in_specs=[VMEM, VMEM, *small_specs, VMEM],
        out_specs=[VMEM] * 5,
        scratch_shapes=[ACC],
        compiler_params=PARAMS,
    )(feats.reshape(per * vb, ch), cotangent.reshape(per * vb, ch), *small, weight_two)
    x_low, x_up, d_low, d_up = exchange(x0, d_lower, d_upper)
    a1, f_own, f_lower, f_upper, grad_w = pl.pallas_call(
        second_kernel,
        out_shape=[
            rows_of(BF16), rows_of(F32), rows_of(BF16), rows_of(BF16),
            jax.ShapeDtypeStruct((kc, ch), F32),
        ],
        in_specs=[VMEM] * 6 + small_specs + [VMEM],
        out_specs=[VMEM] * 5,
        scratch_shapes=[WIN, STACK, ACC],
        compiler_params=PARAMS,
    )(x_low, x0, x_up, d_own, d_up, d_low, *small, weight_one)
    grad_one = lax.psum_scatter(grad_w, "gx", scatter_dimension=0, tiled=True)
    a_low, a_up, f_low, f_up = exchange(a1, f_lower, f_upper)
    block_out, feats_grad = pl.pallas_call(
        third_kernel,
        out_shape=[rows_of(BF16), rows_of(BF16)],
        in_specs=[VMEM] * 8 + small_specs + [VMEM],
        out_specs=[VMEM] * 2,
        scratch_shapes=[WIN, STACK],
        compiler_params=PARAMS,
    )(a_low, a1, a_up, f_own, f_up, f_low, x0, g2, *small, weight_two)
    return (block_out.reshape(per, vb, ch), feats_grad.reshape(per, vb, ch), grad_one)


def solution(mesh):
    split = ("scene", "gx")
    in_specs = (
        P(split, None, None), P(split, None), P(split, None), P(split), P(), P(),
        P(split, None, None),
    )
    out_specs = (P(split, None, None), P(split, None, None), P(split, None))
    return jax.shard_map(
        on_device, mesh=mesh, in_specs=in_specs, out_specs=out_specs, check_vma=False
    )
```

```python
import jax
import jax.numpy as jnp
from jax import lax
from jax.experimental import pallas as pl
from jax.experimental.pallas import tpu as pltpu
from jax.sharding import PartitionSpec as P

F32, BF16 = jnp.float32, jnp.bfloat16
VMEM = pl.BlockSpec(memory_space=pltpu.VMEM)
SMEM = pl.BlockSpec(memory_space=pltpu.SMEM)

ROWS, SIDE = 256, 16


def iota(shape, dim):
    return lax.broadcasted_iota(jnp.int32, shape, dim)


def natural_of(row):
    return ((row >> 2) & 3) * 64 + (row >> 6) * 16 + ((row >> 4) & 3) * 4 + (row & 3)


def to_rows():
    shape = (ROWS, ROWS)
    return (natural_of(iota(shape, 0)) == iota(shape, 1)).astype(F32).astype(BF16)


def from_rows():
    shape = (ROWS, ROWS)
    return (natural_of(iota(shape, 1)) == iota(shape, 0)).astype(F32).astype(BF16)


def mat(a, b):
    return jnp.dot(a, b, preferred_element_type=F32)


def mask_rows(mask_ref, counts_ref):
    row = iota((ROWS, 64), 0)
    brick = (row >> 2) & 3
    held = mask_ref[...].astype(F32)
    spread = jnp.zeros((ROWS, 64), F32)
    for b in range(4):
        spread = jnp.where(brick == b, held[b : b + 1, :], spread)
    keep = (iota((ROWS, 64), 1) == (natural_of(row) & 63)) & (brick < counts_ref[0])
    return jnp.sum(jnp.where(keep, spread, 0.0), axis=1, keepdims=True)


def pickers(table_ref):
    row = iota((128, 27), 0) & 63
    shift, brick, k = row >> 4, (row >> 2) & 3, row & 3
    moved = k + shift - 1
    step = jnp.where(moved < 0, 0, jnp.where(moved > 3, 2, 1))
    held = table_ref[...].astype(F32)
    spread = jnp.zeros((128, 27), F32)
    for b in range(4):
        spread = jnp.where(brick == b, held[b : b + 1, :], spread)
    lane = iota((128, 128), 1)
    wide = iota((128, 128), 0) & 63
    source = ((wide & 3) + (wide >> 4) - 1) & 3
    fits = ((lane & 3) == source) & (wide < 48)
    picks = {}
    for qa in range(3):
        for qb in range(3):
            chosen = iota((128, 27), 1) == qa * 9 + qb * 3 + step
            entry = jnp.sum(jnp.where(chosen, spread, 0.0), axis=1, keepdims=True)
            hit = fits & (entry.astype(jnp.int32) == (lane >> 2)) & (lane < 48)
            picks[qa, qb] = hit.astype(F32)
    return picks


def places():
    for wi in range(6):
        for wj in range(6):
            qa, qb = (wi + 3) // 4, (wj + 3) // 4
            yield wi, wj, (qa, qb), (wi + 3) % 4, (wj + 3) % 4


def gather_windows(picks, lower, own, upper, win):
    half = {key: value[:48, :48].astype(BF16) for key, value in picks.items()}
    for wi, wj, q, i, j in places():
        at = pl.ds((i * 4 + j) * SIDE, SIDE)
        source = jnp.concatenate([lower[at], own[at], upper[at]], 0)
        got = mat(half[q], source).astype(BF16)
        for c in range(3):
            win[c, wi, wj] = got[c * SIDE : (c + 1) * SIDE]


def build_stack(win, stack):
    for o in range(27):
        a, b, c = o // 9, o // 3 % 3, o % 3
        stack[:, o * 256 : (o + 1) * 256] = win[c, a : a + 4, b : b + 4].reshape(ROWS, 256)


def spread_back(picks, grad, weight_ref, acc, own, lower, upper):
    acc[...] = jnp.zeros(acc.shape, F32)
    for o in range(27):
        a, b, c = o // 9, o // 3 % 3, o % 3
        part = lax.dot_general(
            grad,
            weight_ref[o * 256 : (o + 1) * 256, :],
            (((1,), (1,)), ((), ())),
            preferred_element_type=F32,
        )
        acc[c, a : a + 4, b : b + 4] += part.reshape(4, 4, SIDE, 256)
    turned = {key: value.T[:48].astype(BF16) for key, value in picks.items()}
    pad = jnp.zeros((SIDE, 256), BF16)
    totals = {}
    for wi, wj, q, i, j in places():
        held = acc[:, wi, wj].reshape(48, 256)
        high = held.astype(BF16)
        low = (held - high.astype(F32)).astype(BF16)
        got = mat(turned[q], jnp.concatenate([high, pad, low, pad], 0))
        totals[i, j] = totals[i, j] + got if (i, j) in totals else got
    for (i, j), value in totals.items():
        at = pl.ds((i * 4 + j) * SIDE, SIDE)
        lower[at] = value[:16].astype(BF16)
        own[at] = value[16:32]
        upper[at] = value[32:48].astype(BF16)


def first_kernel(feats, cot, mask, table, counts, w2, x0, g2, own, lower, upper, acc):
    keep = mask_rows(mask, counts)
    turn = to_rows()
    x0[...] = (mat(turn, feats[...]) * keep).astype(BF16)
    grad = (mat(turn, cot[...]) * keep).astype(BF16)
    g2[...] = grad
    spread_back(pickers(table), grad, w2, acc, own, lower, upper)


def second_kernel(
    x0_low, x0, x0_up, d_own, d_up, d_low, mask, table, counts, w1,
    a1, own, lower, upper, grad_w, win, stack, acc,
):
    keep = mask_rows(mask, counts)
    picks = pickers(table)
    gather_windows(picks, x0_low, x0, x0_up, win)
    build_stack(win, stack)
    y1 = mat(stack[...], w1[...]) * keep
    sig = 1.0 / (1.0 + jnp.exp(-y1))
    a1[...] = (y1 * sig).astype(BF16)
    da1 = d_own[...] + d_up[...].astype(F32) + d_low[...].astype(F32)
    g1 = (da1 * keep * (sig * (1.0 + y1 * (1.0 - sig)))).astype(BF16)
    for o in range(27):
        at = slice(o * 256, (o + 1) * 256)
        grad_w[at, :] = lax.dot_general(
            stack[:, at], g1, (((0,), (0,)), ((), ())), preferred_element_type=F32
        )
    spread_back(picks, g1, w1, acc, own, lower, upper)


def third_kernel(
    a_low, a1, a_up, f_own, f_up, f_low, x0, g2, mask, table, counts, w2,
    block_out, feats_grad, win, stack,
):
    keep = mask_rows(mask, counts)
    gather_windows(pickers(table), a_low, a1, a_up, win)
    build_stack(win, stack)
    y2 = mat(stack[...], w2[...]) * keep
    out = (y2 + x0[...].astype(F32)).astype(BF16)
    turn = from_rows()
    block_out[...] = mat(turn, out).astype(BF16)
    total = f_own[...] + f_up[...].astype(F32) + f_low[...].astype(F32)
    grad = (keep * (total + g2[...].astype(F32))).astype(BF16)
    feats_grad[...] = mat(turn, grad).astype(BF16)


def peer(z, y, core):
    return {"gx": z * 4 + y * 2 + core}


def remote(source, target, send_sem, recv_sem, device):
    return pltpu.make_async_remote_copy(
        src_ref=source, dst_ref=target, send_sem=send_sem, recv_sem=recv_sem,
        device_id=device, device_id_type=pl.DeviceIdType.MESH,
    )


def reduce_kernel(
    grad, out, to_core, from_core, to_y, from_y, held, to_z, from_z,
    core_send, core_recv, y_send, y_recv, z_send, z_recv,
):
    me = lax.axis_index("gx")
    z, y, core = me // 4, (me // 2) % 2, me % 2
    targets = [(z + 1 + step) % 4 for step in range(4)]
    partners = [peer(z, y, 1 - core), peer(z, 1 - y, core)]
    partners += [peer(target, y, core) for target in targets[:3]]
    barrier = pltpu.get_barrier_semaphore()
    for device in partners:
        pl.semaphore_signal(barrier, inc=1, device_id=device, device_id_type=pl.DeviceIdType.MESH)
    pl.semaphore_wait(barrier, len(partners))
    by_core, by_y, by_z = [], [], []
    for step, target in enumerate(targets):
        for side in range(2):
            to_core[step, side] = grad[target * 4 + side * 2 + 1 - core].astype(BF16)
        copy = remote(
            to_core.at[step], from_core.at[step], core_send.at[step], core_recv.at[step],
            partners[0],
        )
        copy.start()
        by_core.append(copy)
    for step, target in enumerate(targets):
        by_core[step].wait_recv()
        away = grad[target * 4 + (1 - y) * 2 + core] + from_core[step, 1 - y].astype(F32)
        to_y[step] = away.astype(BF16)
        copy = remote(
            to_y.at[step], from_y.at[step], y_send.at[step], y_recv.at[step], partners[1]
        )
        copy.start()
        by_y.append(copy)
        held[step] = grad[target * 4 + y * 2 + core] + from_core[step, y].astype(F32)
    for step in range(3):
        by_y[step].wait_recv()
        to_z[step] = (held[step] + from_y[step].astype(F32)).astype(BF16)
        copy = remote(
            to_z.at[step], from_z.at[step], z_send.at[step], z_recv.at[step], partners[2 + step]
        )
        copy.start()
        by_z.append(copy)
    by_y[3].wait_recv()
    total = held[3] + from_y[3].astype(F32)
    for step in range(3):
        by_z[step].wait_recv()
    out[...] = total + from_z[0].astype(F32) + from_z[1].astype(F32) + from_z[2].astype(F32)
    for copy in by_core + by_y + by_z:
        copy.wait_send()


def reduce_scattered(grad):
    devices = lax.axis_size("gx")
    if devices != 16:
        return lax.psum_scatter(grad, "gx", scatter_dimension=0, tiled=True)
    rows, ch = grad.shape
    share = (rows // devices, ch)
    return pl.pallas_call(
        reduce_kernel,
        out_shape=jax.ShapeDtypeStruct(share, F32),
        in_specs=[VMEM],
        out_specs=VMEM,
        scratch_shapes=[
            pltpu.VMEM((4, 2, *share), BF16),
            pltpu.VMEM((4, 2, *share), BF16),
            pltpu.VMEM((4, *share), BF16),
            pltpu.VMEM((4, *share), BF16),
            pltpu.VMEM((4, *share), F32),
            pltpu.VMEM((3, *share), BF16),
            pltpu.VMEM((3, *share), BF16),
            *[pltpu.SemaphoreType.DMA((4,))] * 4,
            *[pltpu.SemaphoreType.DMA((3,))] * 2,
        ],
        cost_estimate=pl.CostEstimate(
            flops=10**10, bytes_accessed=10**8, transcendentals=0
        ),
        compiler_params=pltpu.CompilerParams(
            vmem_limit_bytes=50 * 2**20, collective_id=0, has_side_effects=True
        ),
    )(grad.reshape(devices, *share))


def rows_of(kind):
    return jax.ShapeDtypeStruct((ROWS, 256), kind)


PARAMS = pltpu.CompilerParams(vmem_limit_bytes=50 * 2**20)
WIN = pltpu.VMEM((3, 6, 6, SIDE, 256), BF16)
ACC = pltpu.VMEM((3, 6, 6, SIDE, 256), F32)
STACK = pltpu.VMEM((ROWS, 6912), BF16)


def shifted(value, steps):
    count = lax.axis_size("gx")
    first, last = (max(0, -steps), min(count, count - steps))
    return lax.ppermute(value, "gx", [(source, source + steps) for source in range(first, last)])


def exchange(field, lower, upper):
    up = shifted(jnp.concatenate([field, upper], 0), 1)
    down = shifted(jnp.concatenate([field, lower], 0), -1)
    return up[:ROWS], down[:ROWS], up[ROWS:], down[ROWS:]


def on_device(feats, voxel_mask, brick_table, counts, weight_one, weight_two, cotangent):
    per, vb, ch = feats.shape
    kc = weight_one.shape[0]
    small = (voxel_mask, brick_table, counts)
    small_specs = [VMEM, VMEM, SMEM]
    x0, g2, d_own, d_lower, d_upper = pl.pallas_call(
        first_kernel,
        out_shape=[rows_of(BF16), rows_of(BF16), rows_of(F32), rows_of(BF16), rows_of(BF16)],
        in_specs=[VMEM, VMEM, *small_specs, VMEM],
        out_specs=[VMEM] * 5,
        scratch_shapes=[ACC],
        compiler_params=PARAMS,
    )(feats.reshape(per * vb, ch), cotangent.reshape(per * vb, ch), *small, weight_two)
    x_low, x_up, d_low, d_up = exchange(x0, d_lower, d_upper)
    a1, f_own, f_lower, f_upper, grad_w = pl.pallas_call(
        second_kernel,
        out_shape=[
            rows_of(BF16), rows_of(F32), rows_of(BF16), rows_of(BF16),
            jax.ShapeDtypeStruct((kc, ch), F32),
        ],
        in_specs=[VMEM] * 6 + small_specs + [VMEM],
        out_specs=[VMEM] * 5,
        scratch_shapes=[WIN, STACK, ACC],
        compiler_params=PARAMS,
    )(x_low, x0, x_up, d_own, d_up, d_low, *small, weight_one)
    grad_one = reduce_scattered(grad_w)
    a_low, a_up, f_low, f_up = exchange(a1, f_lower, f_upper)
    block_out, feats_grad = pl.pallas_call(
        third_kernel,
        out_shape=[rows_of(BF16), rows_of(BF16)],
        in_specs=[VMEM] * 8 + small_specs + [VMEM],
        out_specs=[VMEM] * 2,
        scratch_shapes=[WIN, STACK],
        compiler_params=PARAMS,
    )(a_low, a1, a_up, f_own, f_up, f_low, x0, g2, *small, weight_two)
    return (block_out.reshape(per, vb, ch), feats_grad.reshape(per, vb, ch), grad_one)


def solution(mesh):
    split = ("scene", "gx")
    in_specs = (
        P(split, None, None), P(split, None), P(split, None), P(split), P(), P(),
        P(split, None, None),
    )
    out_specs = (P(split, None, None), P(split, None, None), P(split, None))
    return jax.shard_map(
        on_device, mesh=mesh, in_specs=in_specs, out_specs=out_specs, check_vma=False
    )
```

```python
import jax
import jax.numpy as jnp
from jax import lax
from jax.experimental import pallas as pl
from jax.experimental.pallas import tpu as pltpu
from jax.sharding import PartitionSpec as P

F32, BF16 = jnp.float32, jnp.bfloat16
VMEM = pl.BlockSpec(memory_space=pltpu.VMEM)
SMEM = pl.BlockSpec(memory_space=pltpu.SMEM)

ROWS, SIDE = 256, 16


def iota(shape, dim):
    return lax.broadcasted_iota(jnp.int32, shape, dim)


def natural_of(row):
    return ((row >> 2) & 3) * 64 + (row >> 6) * 16 + ((row >> 4) & 3) * 4 + (row & 3)


def to_rows():
    shape = (ROWS, ROWS)
    return (natural_of(iota(shape, 0)) == iota(shape, 1)).astype(F32).astype(BF16)


def from_rows():
    shape = (ROWS, ROWS)
    return (natural_of(iota(shape, 1)) == iota(shape, 0)).astype(F32).astype(BF16)


def mat(a, b):
    return jnp.dot(a, b, preferred_element_type=F32)


def mask_rows(mask_ref, counts_ref):
    row = iota((ROWS, 64), 0)
    brick = (row >> 2) & 3
    held = mask_ref[...].astype(F32)
    spread = jnp.zeros((ROWS, 64), F32)
    for b in range(4):
        spread = jnp.where(brick == b, held[b : b + 1, :], spread)
    keep = (iota((ROWS, 64), 1) == (natural_of(row) & 63)) & (brick < counts_ref[0])
    return jnp.sum(jnp.where(keep, spread, 0.0), axis=1, keepdims=True)


def pickers(table_ref):
    row = iota((128, 27), 0) & 63
    shift, brick, k = row >> 4, (row >> 2) & 3, row & 3
    moved = k + shift - 1
    step = jnp.where(moved < 0, 0, jnp.where(moved > 3, 2, 1))
    held = table_ref[...].astype(F32)
    spread = jnp.zeros((128, 27), F32)
    for b in range(4):
        spread = jnp.where(brick == b, held[b : b + 1, :], spread)
    lane = iota((128, 128), 1)
    wide = iota((128, 128), 0) & 63
    source = ((wide & 3) + (wide >> 4) - 1) & 3
    fits = ((lane & 3) == source) & (wide < 48)
    picks = {}
    for qa in range(3):
        for qb in range(3):
            chosen = iota((128, 27), 1) == qa * 9 + qb * 3 + step
            entry = jnp.sum(jnp.where(chosen, spread, 0.0), axis=1, keepdims=True)
            hit = fits & (entry.astype(jnp.int32) == (lane >> 2)) & (lane < 48)
            picks[qa, qb] = hit.astype(F32)
    return picks


def places():
    for wi in range(6):
        for wj in range(6):
            qa, qb = (wi + 3) // 4, (wj + 3) // 4
            yield wi, wj, (qa, qb), (wi + 3) % 4, (wj + 3) % 4


def gather_windows(picks, lower, own, upper, win):
    half = {key: value[:48, :48].astype(BF16) for key, value in picks.items()}
    for wi, wj, q, i, j in places():
        at = pl.ds((i * 4 + j) * SIDE, SIDE)
        source = jnp.concatenate([lower[at], own[at], upper[at]], 0)
        got = mat(half[q], source).astype(BF16)
        for c in range(3):
            win[c, wi, wj] = got[c * SIDE : (c + 1) * SIDE]


def build_stack(win, stack):
    for o in range(27):
        a, b, c = o // 9, o // 3 % 3, o % 3
        stack[:, o * 256 : (o + 1) * 256] = win[c, a : a + 4, b : b + 4].reshape(ROWS, 256)


def spread_back(picks, grad, weight_ref, acc, own, lower, upper):
    acc[...] = jnp.zeros(acc.shape, F32)
    for o in range(27):
        a, b, c = o // 9, o // 3 % 3, o % 3
        part = lax.dot_general(
            grad,
            weight_ref[o * 256 : (o + 1) * 256, :],
            (((1,), (1,)), ((), ())),
            preferred_element_type=F32,
        )
        acc[c, a : a + 4, b : b + 4] += part.reshape(4, 4, SIDE, 256)
    turned = {key: value.T[:48].astype(BF16) for key, value in picks.items()}
    pad = jnp.zeros((SIDE, 256), BF16)
    totals = {}
    for wi, wj, q, i, j in places():
        held = acc[:, wi, wj].reshape(48, 256)
        high = held.astype(BF16)
        low = (held - high.astype(F32)).astype(BF16)
        got = mat(turned[q], jnp.concatenate([high, pad, low, pad], 0))
        totals[i, j] = totals[i, j] + got if (i, j) in totals else got
    for (i, j), value in totals.items():
        at = pl.ds((i * 4 + j) * SIDE, SIDE)
        lower[at] = value[:16].astype(BF16)
        own[at] = value[16:32]
        upper[at] = value[32:48].astype(BF16)


def first_kernel(feats, cot, mask, table, counts, w2, x0, g2, own, lower, upper, acc):
    keep = mask_rows(mask, counts)
    turn = to_rows()
    x0[...] = (mat(turn, feats[...]) * keep).astype(BF16)
    grad = (mat(turn, cot[...]) * keep).astype(BF16)
    g2[...] = grad
    spread_back(pickers(table), grad, w2, acc, own, lower, upper)


def second_kernel(
    x0_low, x0, x0_up, d_own, d_up, d_low, mask, table, counts, w1,
    a1, own, lower, upper, grad_w, win, stack, acc,
):
    keep = mask_rows(mask, counts)
    picks = pickers(table)
    gather_windows(picks, x0_low, x0, x0_up, win)
    build_stack(win, stack)
    y1 = mat(stack[...], w1[...]) * keep
    sig = 1.0 / (1.0 + jnp.exp(-y1))
    a1[...] = (y1 * sig).astype(BF16)
    da1 = d_own[...] + d_up[...].astype(F32) + d_low[...].astype(F32)
    g1 = (da1 * keep * (sig * (1.0 + y1 * (1.0 - sig)))).astype(BF16)
    for o in range(27):
        at = slice(o * 256, (o + 1) * 256)
        grad_w[at, :] = lax.dot_general(
            stack[:, at], g1, (((0,), (0,)), ((), ())), preferred_element_type=F32
        )
    spread_back(picks, g1, w1, acc, own, lower, upper)


def third_kernel(
    a_low, a1, a_up, f_own, f_up, f_low, x0, g2, mask, table, counts, w2,
    block_out, feats_grad, win, stack,
):
    keep = mask_rows(mask, counts)
    gather_windows(pickers(table), a_low, a1, a_up, win)
    build_stack(win, stack)
    y2 = mat(stack[...], w2[...]) * keep
    out = (y2 + x0[...].astype(F32)).astype(BF16)
    turn = from_rows()
    block_out[...] = mat(turn, out).astype(BF16)
    total = f_own[...] + f_up[...].astype(F32) + f_low[...].astype(F32)
    grad = (keep * (total + g2[...].astype(F32))).astype(BF16)
    feats_grad[...] = mat(turn, grad).astype(BF16)


def peer(z, y, core):
    return {"gx": z * 4 + y * 2 + core}


def remote(source, target, send_sem, recv_sem, device):
    return pltpu.make_async_remote_copy(
        src_ref=source, dst_ref=target, send_sem=send_sem, recv_sem=recv_sem,
        device_id=device, device_id_type=pl.DeviceIdType.MESH,
    )


def rows_of(kind):
    return jax.ShapeDtypeStruct((ROWS, 256), kind)


PARAMS = pltpu.CompilerParams(vmem_limit_bytes=50 * 2**20)
WIN = pltpu.VMEM((3, 6, 6, SIDE, 256), BF16)
ACC = pltpu.VMEM((3, 6, 6, SIDE, 256), F32)
STACK = pltpu.VMEM((ROWS, 6912), BF16)


def shifted(value, steps):
    count = lax.axis_size("gx")
    first, last = (max(0, -steps), min(count, count - steps))
    return lax.ppermute(value, "gx", [(source, source + steps) for source in range(first, last)])


def exchange(field, lower, upper):
    up = shifted(jnp.concatenate([field, upper], 0), 1)
    down = shifted(jnp.concatenate([field, lower], 0), -1)
    return up[:ROWS], down[:ROWS], up[ROWS:], down[ROWS:]


def whole_kernel(
    feats, cot, mask, table, counts, w1_hbm, w2_hbm,
    block_out, feats_grad, grad_out,
    w1, w2, win, stack, acc, g2, own, grad, field, from_low, from_up, down_sum, up_sum,
    sum_low, sum_up, to_core, from_core, to_y, from_y, held, to_z, from_z,
    load, ring_send, ring_recv, sum_send, sum_recv,
    core_send, core_recv, y_send, y_recv, z_send, z_recv,
):
    me, devices, share = lax.axis_index("gx"), lax.axis_size("gx"), grad_out.shape[0]
    z, y, core = me // 4, (me // 2) % 2, me % 2
    targets = [(z + 1 + step) % 4 for step in range(4)]
    partners = [peer(z, y, 1 - core), peer(z, 1 - y, core)]
    partners += [peer(target, y, core) for target in targets[:3]]
    other = {"gx": (me + 2 * core - 1 + devices) % devices}
    above, below = {"gx": (me + 1) % devices}, {"gx": (me - 1 + devices) % devices}
    barrier = pltpu.get_barrier_semaphore()
    for device in [*partners, other]:
        pl.semaphore_signal(barrier, inc=1, device_id=device, device_id_type=pl.DeviceIdType.MESH)
    load_w2 = pltpu.make_async_copy(w2_hbm, w2, load.at[0])
    load_w1 = pltpu.make_async_copy(w1_hbm, w1, load.at[1])
    load_w2.start()
    load_w1.start()
    has_above, has_below = me < devices - 1, me > 0

    @pl.when(me == 0)
    def _():
        from_low[...] = jnp.zeros(from_low.shape, BF16)
        sum_low[...] = jnp.zeros(sum_low.shape, BF16)

    @pl.when(me == devices - 1)
    def _():
        from_up[...] = jnp.zeros(from_up.shape, BF16)
        sum_up[...] = jnp.zeros(sum_up.shape, BF16)

    def ring(n, up_source, low_slot, down_source, up_slot, send, recv):
        return (
            remote(up_source.at[n], low_slot.at[n], send.at[n, 0], recv.at[n, 0], above),
            remote(down_source.at[n], up_slot.at[n], send.at[n, 1], recv.at[n, 1], below),
        )

    def start(pair):
        pl.when(has_above)(pair[0].start)
        pl.when(has_below)(pair[1].start)

    def wait_recv(pair):
        pl.when(has_below)(pair[0].wait_recv)
        pl.when(has_above)(pair[1].wait_recv)

    def wait_send(pair):
        pl.when(has_above)(pair[0].wait_send)
        pl.when(has_below)(pair[1].wait_send)

    fields = [ring(n, field, from_low, field, from_up, ring_send, ring_recv) for n in range(2)]
    sums = [ring(n, up_sum, sum_low, down_sum, sum_up, sum_send, sum_recv) for n in range(2)]

    keep = mask_rows(mask, counts)
    turn = to_rows()
    field[0] = (mat(turn, feats[...]) * keep).astype(BF16)
    pl.semaphore_wait(barrier, len(partners) + 1)
    start(fields[0])
    g2[...] = (mat(turn, cot[...]) * keep).astype(BF16)
    picks = pickers(table)
    load_w2.wait()
    spread_back(picks, g2[...], w2, acc, own, down_sum.at[0], up_sum.at[0])
    start(sums[0])
    load_w1.wait()
    wait_recv(fields[0])
    gather_windows(picks, from_low.at[0], field.at[0], from_up.at[0], win)
    build_stack(win, stack)
    y1 = mat(stack[...], w1[...]) * keep
    sig = 1.0 / (1.0 + jnp.exp(-y1))
    field[1] = (y1 * sig).astype(BF16)
    start(fields[1])
    wait_recv(sums[0])
    da1 = own[...] + sum_up[0].astype(F32) + sum_low[0].astype(F32)
    g1 = (da1 * keep * (sig * (1.0 + y1 * (1.0 - sig)))).astype(BF16)
    for o in range(27):
        at = slice(o * 256, (o + 1) * 256)
        grad[at, :] = lax.dot_general(
            stack[:, at], g1, (((0,), (0,)), ((), ())), preferred_element_type=F32
        )

    def part(target, side, half):
        first = pl.multiple_of((target * 4 + side * 2 + half) * share, 16)
        return grad[pl.ds(first, share), :]

    by_core, by_y, by_z = [], [], []
    for step, target in enumerate(targets):
        for side in range(2):
            to_core[step, side] = part(target, side, 1 - core).astype(BF16)
        copy = remote(
            to_core.at[step], from_core.at[step], core_send.at[step], core_recv.at[step],
            partners[0],
        )
        copy.start()
        by_core.append(copy)

    def core_to_y(step):
        by_core[step].wait_recv()
        target = targets[step]
        away = part(target, 1 - y, core) + from_core[step, 1 - y].astype(F32)
        to_y[step] = away.astype(BF16)
        copy = remote(
            to_y.at[step], from_y.at[step], y_send.at[step], y_recv.at[step], partners[1]
        )
        copy.start()
        by_y.append(copy)
        held[step] = part(target, y, core) + from_core[step, y].astype(F32)

    def y_to_z(step):
        by_y[step].wait_recv()
        to_z[step] = (held[step] + from_y[step].astype(F32)).astype(BF16)
        copy = remote(
            to_z.at[step], from_z.at[step], z_send.at[step], z_recv.at[step], partners[2 + step]
        )
        copy.start()
        by_z.append(copy)

    core_to_y(0)
    core_to_y(1)
    spread_back(picks, g1, w1, acc, own, down_sum.at[1], up_sum.at[1])
    start(sums[1])
    core_to_y(2)
    core_to_y(3)
    y_to_z(0)
    wait_recv(fields[1])
    gather_windows(picks, from_low.at[1], field.at[1], from_up.at[1], win)
    build_stack(win, stack)
    y_to_z(1)
    y2 = mat(stack[...], w2[...]) * keep
    out = (y2 + field[0].astype(F32)).astype(BF16)
    turn = from_rows()
    block_out[...] = mat(turn, out).astype(BF16)
    y_to_z(2)
    wait_recv(sums[1])
    total = own[...] + sum_up[1].astype(F32) + sum_low[1].astype(F32)
    back = (keep * (total + g2[...].astype(F32))).astype(BF16)
    feats_grad[...] = mat(turn, back).astype(BF16)
    by_y[3].wait_recv()
    grad_out[...] = held[3] + from_y[3].astype(F32)
    for step in range(3):
        by_z[step].wait_recv()
        grad_out[...] += from_z[step].astype(F32)
    for copy in by_core + by_y + by_z:
        copy.wait_send()
    for pair in fields + sums:
        wait_send(pair)


def in_one(feats, voxel_mask, brick_table, counts, weight_one, weight_two, cotangent):
    per, vb, ch = feats.shape
    share = (weight_one.shape[0] // lax.axis_size("gx"), ch)
    anywhere = pl.BlockSpec(memory_space=pl.ANY)
    pair = pltpu.VMEM((2, ROWS, ch), BF16)
    block_out, feats_grad, grad_one = pl.pallas_call(
        whole_kernel,
        out_shape=[rows_of(BF16), rows_of(BF16), jax.ShapeDtypeStruct(share, F32)],
        in_specs=[VMEM, VMEM, VMEM, VMEM, SMEM, anywhere, anywhere],
        out_specs=[VMEM] * 3,
        scratch_shapes=[
            pltpu.VMEM(weight_one.shape, BF16),
            pltpu.VMEM(weight_two.shape, BF16),
            WIN,
            STACK,
            ACC,
            pltpu.VMEM((ROWS, ch), BF16),
            pltpu.VMEM((ROWS, ch), F32),
            pltpu.VMEM(weight_one.shape, F32),
            *[pair] * 7,
            pltpu.VMEM((4, 2, *share), BF16),
            pltpu.VMEM((4, 2, *share), BF16),
            pltpu.VMEM((4, *share), BF16),
            pltpu.VMEM((4, *share), BF16),
            pltpu.VMEM((4, *share), F32),
            pltpu.VMEM((3, *share), BF16),
            pltpu.VMEM((3, *share), BF16),
            pltpu.SemaphoreType.DMA((2,)),
            *[pltpu.SemaphoreType.DMA((2, 2))] * 4,
            *[pltpu.SemaphoreType.DMA((4,))] * 4,
            *[pltpu.SemaphoreType.DMA((3,))] * 2,
        ],
        compiler_params=pltpu.CompilerParams(
            vmem_limit_bytes=56 * 2**20, collective_id=0, has_side_effects=True
        ),
    )(
        feats.reshape(per * vb, ch), cotangent.reshape(per * vb, ch), voxel_mask, brick_table,
        counts, weight_one, weight_two,
    )
    return (block_out.reshape(per, vb, ch), feats_grad.reshape(per, vb, ch), grad_one)


def on_device(feats, voxel_mask, brick_table, counts, weight_one, weight_two, cotangent):
    if lax.axis_size("gx") == 16:
        return in_one(feats, voxel_mask, brick_table, counts, weight_one, weight_two, cotangent)
    per, vb, ch = feats.shape
    kc = weight_one.shape[0]
    small = (voxel_mask, brick_table, counts)
    small_specs = [VMEM, VMEM, SMEM]
    x0, g2, d_own, d_lower, d_upper = pl.pallas_call(
        first_kernel,
        out_shape=[rows_of(BF16), rows_of(BF16), rows_of(F32), rows_of(BF16), rows_of(BF16)],
        in_specs=[VMEM, VMEM, *small_specs, VMEM],
        out_specs=[VMEM] * 5,
        scratch_shapes=[ACC],
        compiler_params=PARAMS,
    )(feats.reshape(per * vb, ch), cotangent.reshape(per * vb, ch), *small, weight_two)
    x_low, x_up, d_low, d_up = exchange(x0, d_lower, d_upper)
    a1, f_own, f_lower, f_upper, grad_w = pl.pallas_call(
        second_kernel,
        out_shape=[
            rows_of(BF16), rows_of(F32), rows_of(BF16), rows_of(BF16),
            jax.ShapeDtypeStruct((kc, ch), F32),
        ],
        in_specs=[VMEM] * 6 + small_specs + [VMEM],
        out_specs=[VMEM] * 5,
        scratch_shapes=[WIN, STACK, ACC],
        compiler_params=PARAMS,
    )(x_low, x0, x_up, d_own, d_up, d_low, *small, weight_one)
    grad_one = lax.psum_scatter(grad_w, "gx", scatter_dimension=0, tiled=True)
    a_low, a_up, f_low, f_up = exchange(a1, f_lower, f_upper)
    block_out, feats_grad = pl.pallas_call(
        third_kernel,
        out_shape=[rows_of(BF16), rows_of(BF16)],
        in_specs=[VMEM] * 8 + small_specs + [VMEM],
        out_specs=[VMEM] * 2,
        scratch_shapes=[WIN, STACK],
        compiler_params=PARAMS,
    )(a_low, a1, a_up, f_own, f_up, f_low, x0, g2, *small, weight_two)
    return (block_out.reshape(per, vb, ch), feats_grad.reshape(per, vb, ch), grad_one)


def solution(mesh):
    split = ("scene", "gx")
    in_specs = (
        P(split, None, None), P(split, None), P(split, None), P(split), P(), P(),
        P(split, None, None),
    )
    out_specs = (P(split, None, None), P(split, None, None), P(split, None))
    return jax.shard_map(
        on_device, mesh=mesh, in_specs=in_specs, out_specs=out_specs, check_vma=False
    )
```

```python
import jax
import jax.numpy as jnp
from jax import lax
from jax.experimental import pallas as pl
from jax.experimental.pallas import tpu as pltpu
from jax.sharding import PartitionSpec as P

F32, BF16 = jnp.float32, jnp.bfloat16
VMEM = pl.BlockSpec(memory_space=pltpu.VMEM)
SMEM = pl.BlockSpec(memory_space=pltpu.SMEM)

ROWS, SIDE = 256, 16


def iota(shape, dim):
    return lax.broadcasted_iota(jnp.int32, shape, dim)


def natural_of(row):
    return ((row >> 2) & 3) * 64 + (row >> 6) * 16 + ((row >> 4) & 3) * 4 + (row & 3)


def to_rows():
    shape = (ROWS, ROWS)
    return (natural_of(iota(shape, 0)) == iota(shape, 1)).astype(F32).astype(BF16)


def from_rows():
    shape = (ROWS, ROWS)
    return (natural_of(iota(shape, 1)) == iota(shape, 0)).astype(F32).astype(BF16)


def mat(a, b):
    return jnp.dot(a, b, preferred_element_type=F32)


def mask_rows(mask_ref, counts_ref):
    row = iota((ROWS, 64), 0)
    brick = (row >> 2) & 3
    held = mask_ref[...].astype(F32)
    spread = jnp.zeros((ROWS, 64), F32)
    for b in range(4):
        spread = jnp.where(brick == b, held[b : b + 1, :], spread)
    keep = (iota((ROWS, 64), 1) == (natural_of(row) & 63)) & (brick < counts_ref[0])
    return jnp.sum(jnp.where(keep, spread, 0.0), axis=1, keepdims=True)


def pickers(table_ref):
    row = iota((128, 27), 0) & 63
    shift, brick, k = row >> 4, (row >> 2) & 3, row & 3
    moved = k + shift - 1
    step = jnp.where(moved < 0, 0, jnp.where(moved > 3, 2, 1))
    held = table_ref[...].astype(F32)
    spread = jnp.zeros((128, 27), F32)
    for b in range(4):
        spread = jnp.where(brick == b, held[b : b + 1, :], spread)
    lane = iota((128, 128), 1)
    wide = iota((128, 128), 0) & 63
    source = ((wide & 3) + (wide >> 4) - 1) & 3
    fits = ((lane & 3) == source) & (wide < 48)
    picks = {}
    for qa in range(3):
        for qb in range(3):
            chosen = iota((128, 27), 1) == qa * 9 + qb * 3 + step
            entry = jnp.sum(jnp.where(chosen, spread, 0.0), axis=1, keepdims=True)
            hit = fits & (entry.astype(jnp.int32) == (lane >> 2)) & (lane < 48)
            picks[qa, qb] = hit.astype(F32)
    return picks


def places():
    for wi in range(6):
        for wj in range(6):
            qa, qb = (wi + 3) // 4, (wj + 3) // 4
            yield wi, wj, (qa, qb), (wi + 3) % 4, (wj + 3) % 4


def gather_windows(picks, lower, own, upper, win):
    half = {key: value[:48, :48].astype(BF16) for key, value in picks.items()}
    for wi, wj, q, i, j in places():
        at = pl.ds((i * 4 + j) * SIDE, SIDE)
        source = jnp.concatenate([lower[at], own[at], upper[at]], 0)
        got = mat(half[q], source).astype(BF16)
        for c in range(3):
            win[c, wi, wj] = got[c * SIDE : (c + 1) * SIDE]


def build_stack(win, stack):
    for o in range(27):
        a, b, c = o // 9, o // 3 % 3, o % 3
        stack[:, o * 256 : (o + 1) * 256] = win[c, a : a + 4, b : b + 4].reshape(ROWS, 256)


def spread_back(picks, grad, weight_ref, acc, own, lower, upper):
    acc[...] = jnp.zeros(acc.shape, F32)
    for o in range(27):
        a, b, c = o // 9, o // 3 % 3, o % 3
        part = lax.dot_general(
            grad,
            weight_ref[o * 256 : (o + 1) * 256, :],
            (((1,), (1,)), ((), ())),
            preferred_element_type=F32,
        )
        acc[c, a : a + 4, b : b + 4] += part.reshape(4, 4, SIDE, 256)
    turned = {key: value.T[:48].astype(BF16) for key, value in picks.items()}
    pad = jnp.zeros((SIDE, 256), BF16)
    totals = {}
    for wi, wj, q, i, j in places():
        held = acc[:, wi, wj].reshape(48, 256)
        high = held.astype(BF16)
        low = (held - high.astype(F32)).astype(BF16)
        got = mat(turned[q], jnp.concatenate([high, pad, low, pad], 0))
        totals[i, j] = totals[i, j] + got if (i, j) in totals else got
    for (i, j), value in totals.items():
        at = pl.ds((i * 4 + j) * SIDE, SIDE)
        lower[at] = value[:16].astype(BF16)
        own[at] = value[16:32]
        upper[at] = value[32:48].astype(BF16)


def first_kernel(feats, cot, mask, table, counts, w2, x0, g2, own, lower, upper, acc):
    keep = mask_rows(mask, counts)
    turn = to_rows()
    x0[...] = (mat(turn, feats[...]) * keep).astype(BF16)
    grad = (mat(turn, cot[...]) * keep).astype(BF16)
    g2[...] = grad
    spread_back(pickers(table), grad, w2, acc, own, lower, upper)


def second_kernel(
    x0_low, x0, x0_up, d_own, d_up, d_low, mask, table, counts, w1,
    a1, own, lower, upper, grad_w, win, stack, acc,
):
    keep = mask_rows(mask, counts)
    picks = pickers(table)
    gather_windows(picks, x0_low, x0, x0_up, win)
    build_stack(win, stack)
    y1 = mat(stack[...], w1[...]) * keep
    sig = 1.0 / (1.0 + jnp.exp(-y1))
    a1[...] = (y1 * sig).astype(BF16)
    da1 = d_own[...] + d_up[...].astype(F32) + d_low[...].astype(F32)
    g1 = (da1 * keep * (sig * (1.0 + y1 * (1.0 - sig)))).astype(BF16)
    for o in range(27):
        at = slice(o * 256, (o + 1) * 256)
        grad_w[at, :] = lax.dot_general(
            stack[:, at], g1, (((0,), (0,)), ((), ())), preferred_element_type=F32
        )
    spread_back(picks, g1, w1, acc, own, lower, upper)


def third_kernel(
    a_low, a1, a_up, f_own, f_up, f_low, x0, g2, mask, table, counts, w2,
    block_out, feats_grad, win, stack,
):
    keep = mask_rows(mask, counts)
    gather_windows(pickers(table), a_low, a1, a_up, win)
    build_stack(win, stack)
    y2 = mat(stack[...], w2[...]) * keep
    out = (y2 + x0[...].astype(F32)).astype(BF16)
    turn = from_rows()
    block_out[...] = mat(turn, out).astype(BF16)
    total = f_own[...] + f_up[...].astype(F32) + f_low[...].astype(F32)
    grad = (keep * (total + g2[...].astype(F32))).astype(BF16)
    feats_grad[...] = mat(turn, grad).astype(BF16)


def peer(z, y, core):
    return {"gx": z * 4 + y * 2 + core}


def remote(source, target, send_sem, recv_sem, device):
    return pltpu.make_async_remote_copy(
        src_ref=source, dst_ref=target, send_sem=send_sem, recv_sem=recv_sem,
        device_id=device, device_id_type=pl.DeviceIdType.MESH,
    )


def rows_of(kind):
    return jax.ShapeDtypeStruct((ROWS, 256), kind)


PARAMS = pltpu.CompilerParams(vmem_limit_bytes=50 * 2**20)
WIN = pltpu.VMEM((3, 6, 6, SIDE, 256), BF16)
ACC = pltpu.VMEM((3, 6, 6, SIDE, 256), F32)
STACK = pltpu.VMEM((ROWS, 6912), BF16)


def shifted(value, steps):
    count = lax.axis_size("gx")
    first, last = (max(0, -steps), min(count, count - steps))
    return lax.ppermute(value, "gx", [(source, source + steps) for source in range(first, last)])


def exchange(field, lower, upper):
    up = shifted(jnp.concatenate([field, upper], 0), 1)
    down = shifted(jnp.concatenate([field, lower], 0), -1)
    return up[:ROWS], down[:ROWS], up[ROWS:], down[ROWS:]


def whole_kernel(
    feats, cot, mask, table, counts, w1_hbm, w2_hbm,
    block_out, feats_grad, grad_out,
    w1, w2, win, stack, acc, g2, own, grad, field, from_low, from_up, down_sum, up_sum,
    sum_low, sum_up, to_core, from_core, to_y, from_y, held, to_z, from_z,
    load, ring_send, ring_recv, sum_send, sum_recv,
    core_send, core_recv, y_send, y_recv, z_send, z_recv,
):
    me, devices, share = lax.axis_index("gx"), lax.axis_size("gx"), grad_out.shape[0]
    z, y, core = me // 4, (me // 2) % 2, me % 2
    targets = [(z + 1 + step) % 4 for step in range(4)]
    partners = [peer(z, y, 1 - core), peer(z, 1 - y, core)]
    partners += [peer(target, y, core) for target in targets[:3]]
    other = {"gx": (me + 2 * core - 1 + devices) % devices}
    above, below = {"gx": (me + 1) % devices}, {"gx": (me - 1 + devices) % devices}
    barrier = pltpu.get_barrier_semaphore()
    for device in [*partners, other]:
        pl.semaphore_signal(barrier, inc=1, device_id=device, device_id_type=pl.DeviceIdType.MESH)
    load_w2 = pltpu.make_async_copy(w2_hbm, w2, load.at[0])
    load_w1 = pltpu.make_async_copy(w1_hbm, w1, load.at[1])
    load_w2.start()
    load_w1.start()
    has_above, has_below = me < devices - 1, me > 0

    @pl.when(me == 0)
    def _():
        from_low[...] = jnp.zeros(from_low.shape, BF16)
        sum_low[...] = jnp.zeros(sum_low.shape, BF16)

    @pl.when(me == devices - 1)
    def _():
        from_up[...] = jnp.zeros(from_up.shape, BF16)
        sum_up[...] = jnp.zeros(sum_up.shape, BF16)

    def ring(n, up_source, low_slot, down_source, up_slot, send, recv):
        return (
            remote(up_source.at[n], low_slot.at[n], send.at[n, 0], recv.at[n, 0], above),
            remote(down_source.at[n], up_slot.at[n], send.at[n, 1], recv.at[n, 1], below),
        )

    def start(pair):
        pl.when(has_above)(pair[0].start)
        pl.when(has_below)(pair[1].start)

    def wait_recv(pair):
        pl.when(has_below)(pair[0].wait_recv)
        pl.when(has_above)(pair[1].wait_recv)

    def wait_send(pair):
        pl.when(has_above)(pair[0].wait_send)
        pl.when(has_below)(pair[1].wait_send)

    fields = [ring(n, field, from_low, field, from_up, ring_send, ring_recv) for n in range(2)]
    sums = [ring(n, up_sum, sum_low, down_sum, sum_up, sum_send, sum_recv) for n in range(2)]

    keep = mask_rows(mask, counts)
    turn = to_rows()
    field[0] = (mat(turn, feats[...]) * keep).astype(BF16)
    pl.semaphore_wait(barrier, len(partners) + 1)
    start(fields[0])
    g2[...] = (mat(turn, cot[...]) * keep).astype(BF16)
    picks = pickers(table)
    load_w2.wait()
    spread_back(picks, g2[...], w2, acc, own, down_sum.at[0], up_sum.at[0])
    start(sums[0])
    load_w1.wait()
    wait_recv(fields[0])
    gather_windows(picks, from_low.at[0], field.at[0], from_up.at[0], win)
    build_stack(win, stack)
    y1 = mat(stack[...], w1[...]) * keep
    sig = 1.0 / (1.0 + jnp.exp(-y1))
    field[1] = (y1 * sig).astype(BF16)
    start(fields[1])
    wait_recv(sums[0])
    da1 = own[...] + sum_up[0].astype(F32) + sum_low[0].astype(F32)
    g1 = (da1 * keep * (sig * (1.0 + y1 * (1.0 - sig)))).astype(BF16)
    half = share // 32 * 16
    pieces = [(0, half), (half, share - half)]

    def part(target, side, lane, first, size):
        start_row = (target * 4 + side * 2 + lane) * share + first
        return grad[pl.ds(pl.multiple_of(start_row, 16), size), :]

    by_core, by_y, by_z = [], [], []

    def grad_to_core(step):
        target = targets[step]
        first = target * 27 // 4 - target // 3
        for n in range(8):
            at = pl.ds(pl.multiple_of((first + n) * 256, 256), 256)
            grad[at, :] = lax.dot_general(
                stack[:, at], g1, (((0,), (0,)), ((), ())), preferred_element_type=F32
            )
        for side in range(2):
            to_core[step, side] = part(target, side, 1 - core, 0, share).astype(BF16)
        copy = remote(
            to_core.at[step], from_core.at[step], core_send.at[step], core_recv.at[step],
            partners[0],
        )
        copy.start()
        by_core.append(copy)

    def core_to_y(step):
        by_core[step].wait_recv()
        target = targets[step]
        for n, (first, size) in enumerate(pieces):
            at = pl.ds(first, size)
            away = part(target, 1 - y, core, first, size)
            to_y[step, at] = (away + from_core[step, 1 - y, at].astype(F32)).astype(BF16)
            copy = remote(
                to_y.at[step, at], from_y.at[step, at], y_send.at[step, n], y_recv.at[step, n],
                partners[1],
            )
            copy.start()
            by_y.append(copy)
        held[step] = part(target, y, core, 0, share) + from_core[step, y].astype(F32)

    def y_to_z(step, n):
        by_y[2 * step + n].wait_recv()
        at = pl.ds(*pieces[n])
        to_z[step, at] = (held[step, at] + from_y[step, at].astype(F32)).astype(BF16)
        copy = remote(
            to_z.at[step, at], from_z.at[step, at], z_send.at[step, n], z_recv.at[step, n],
            partners[2 + step],
        )
        copy.start()
        by_z.append(copy)

    grad_to_core(0)
    grad_to_core(1)
    core_to_y(0)
    grad_to_core(2)
    core_to_y(1)
    grad_to_core(3)
    core_to_y(2)
    core_to_y(3)
    y_to_z(0, 0)
    spread_back(picks, g1, w1, acc, own, down_sum.at[1], up_sum.at[1])
    y_to_z(0, 1)
    start(sums[1])
    wait_recv(fields[1])
    gather_windows(picks, from_low.at[1], field.at[1], from_up.at[1], win)
    build_stack(win, stack)
    y_to_z(1, 0)
    y2 = mat(stack[...], w2[...]) * keep
    block_out[...] = (y2 + field[0].astype(F32)).astype(BF16)
    y_to_z(1, 1)
    y_to_z(2, 0)
    y_to_z(2, 1)
    wait_recv(sums[1])
    total = own[...] + sum_up[1].astype(F32) + sum_low[1].astype(F32)
    feats_grad[...] = (keep * (total + g2[...].astype(F32))).astype(BF16)
    by_y[6].wait_recv()
    by_y[7].wait_recv()
    grad_out[...] = held[3] + from_y[3].astype(F32)
    for step in range(3):
        by_z[2 * step].wait_recv()
        by_z[2 * step + 1].wait_recv()
        grad_out[...] += from_z[step].astype(F32)
    for copy in by_core + by_y + by_z:
        copy.wait_send()
    for pair in fields + sums:
        wait_send(pair)


def last_kernel(block_rows, grad_rows, share, block_out, feats_grad, grad_out):
    turn = from_rows()
    block_out[...] = mat(turn, block_rows[...]).astype(BF16)
    feats_grad[...] = mat(turn, grad_rows[...]).astype(BF16)
    grad_out[...] = share[...]


def in_one(feats, voxel_mask, brick_table, counts, weight_one, weight_two, cotangent):
    per, vb, ch = feats.shape
    share = (weight_one.shape[0] // lax.axis_size("gx"), ch)
    anywhere = pl.BlockSpec(memory_space=pl.ANY)
    pair = pltpu.VMEM((2, ROWS, ch), BF16)
    shapes = [rows_of(BF16), rows_of(BF16), jax.ShapeDtypeStruct(share, F32)]
    parts = pl.pallas_call(
        whole_kernel,
        out_shape=shapes,
        in_specs=[VMEM, VMEM, VMEM, VMEM, SMEM, anywhere, anywhere],
        out_specs=[VMEM] * 3,
        scratch_shapes=[
            pltpu.VMEM(weight_one.shape, BF16),
            pltpu.VMEM(weight_two.shape, BF16),
            WIN,
            STACK,
            ACC,
            pltpu.VMEM((ROWS, ch), BF16),
            pltpu.VMEM((ROWS, ch), F32),
            pltpu.VMEM(weight_one.shape, F32),
            *[pair] * 7,
            pltpu.VMEM((4, 2, *share), BF16),
            pltpu.VMEM((4, 2, *share), BF16),
            pltpu.VMEM((4, *share), BF16),
            pltpu.VMEM((4, *share), BF16),
            pltpu.VMEM((4, *share), F32),
            pltpu.VMEM((3, *share), BF16),
            pltpu.VMEM((3, *share), BF16),
            pltpu.SemaphoreType.DMA((2,)),
            *[pltpu.SemaphoreType.DMA((2, 2))] * 4,
            *[pltpu.SemaphoreType.DMA((4,))] * 2,
            *[pltpu.SemaphoreType.DMA((4, 2))] * 2,
            *[pltpu.SemaphoreType.DMA((3, 2))] * 2,
        ],
        compiler_params=pltpu.CompilerParams(
            vmem_limit_bytes=56 * 2**20, collective_id=0, has_side_effects=True
        ),
    )(
        feats.reshape(per * vb, ch), cotangent.reshape(per * vb, ch), voxel_mask, brick_table,
        counts, weight_one, weight_two,
    )
    block_out, feats_grad, grad_one = pl.pallas_call(
        last_kernel, out_shape=shapes, in_specs=[VMEM] * 3, out_specs=[VMEM] * 3,
        compiler_params=pltpu.CompilerParams(vmem_limit_bytes=60 * 2**20),
    )(*parts)
    return (block_out.reshape(per, vb, ch), feats_grad.reshape(per, vb, ch), grad_one)


def on_device(feats, voxel_mask, brick_table, counts, weight_one, weight_two, cotangent):
    if lax.axis_size("gx") == 16:
        return in_one(feats, voxel_mask, brick_table, counts, weight_one, weight_two, cotangent)
    per, vb, ch = feats.shape
    kc = weight_one.shape[0]
    small = (voxel_mask, brick_table, counts)
    small_specs = [VMEM, VMEM, SMEM]
    x0, g2, d_own, d_lower, d_upper = pl.pallas_call(
        first_kernel,
        out_shape=[rows_of(BF16), rows_of(BF16), rows_of(F32), rows_of(BF16), rows_of(BF16)],
        in_specs=[VMEM, VMEM, *small_specs, VMEM],
        out_specs=[VMEM] * 5,
        scratch_shapes=[ACC],
        compiler_params=PARAMS,
    )(feats.reshape(per * vb, ch), cotangent.reshape(per * vb, ch), *small, weight_two)
    x_low, x_up, d_low, d_up = exchange(x0, d_lower, d_upper)
    a1, f_own, f_lower, f_upper, grad_w = pl.pallas_call(
        second_kernel,
        out_shape=[
            rows_of(BF16), rows_of(F32), rows_of(BF16), rows_of(BF16),
            jax.ShapeDtypeStruct((kc, ch), F32),
        ],
        in_specs=[VMEM] * 6 + small_specs + [VMEM],
        out_specs=[VMEM] * 5,
        scratch_shapes=[WIN, STACK, ACC],
        compiler_params=PARAMS,
    )(x_low, x0, x_up, d_own, d_up, d_low, *small, weight_one)
    grad_one = lax.psum_scatter(grad_w, "gx", scatter_dimension=0, tiled=True)
    a_low, a_up, f_low, f_up = exchange(a1, f_lower, f_upper)
    block_out, feats_grad = pl.pallas_call(
        third_kernel,
        out_shape=[rows_of(BF16), rows_of(BF16)],
        in_specs=[VMEM] * 8 + small_specs + [VMEM],
        out_specs=[VMEM] * 2,
        scratch_shapes=[WIN, STACK],
        compiler_params=PARAMS,
    )(a_low, a1, a_up, f_own, f_up, f_low, x0, g2, *small, weight_two)
    return (block_out.reshape(per, vb, ch), feats_grad.reshape(per, vb, ch), grad_one)


def solution(mesh):
    split = ("scene", "gx")
    in_specs = (
        P(split, None, None), P(split, None), P(split, None), P(split), P(), P(),
        P(split, None, None),
    )
    out_specs = (P(split, None, None), P(split, None, None), P(split, None))
    return jax.shard_map(
        on_device, mesh=mesh, in_specs=in_specs, out_specs=out_specs, check_vma=False
    )
```

```python
import jax
import jax.numpy as jnp
from jax import lax
from jax.experimental import pallas as pl
from jax.experimental.pallas import tpu as pltpu
from jax.sharding import PartitionSpec as P

F32, BF16 = jnp.float32, jnp.bfloat16
VMEM = pl.BlockSpec(memory_space=pltpu.VMEM)
SMEM = pl.BlockSpec(memory_space=pltpu.SMEM)

ROWS, SIDE = 256, 16


def iota(shape, dim):
    return lax.broadcasted_iota(jnp.int32, shape, dim)


def natural_of(row):
    return ((row >> 2) & 3) * 64 + (row >> 6) * 16 + ((row >> 4) & 3) * 4 + (row & 3)


def to_rows():
    shape = (ROWS, ROWS)
    return (natural_of(iota(shape, 0)) == iota(shape, 1)).astype(F32).astype(BF16)


def from_rows():
    shape = (ROWS, ROWS)
    return (natural_of(iota(shape, 1)) == iota(shape, 0)).astype(F32).astype(BF16)


def mat(a, b):
    return jnp.dot(a, b, preferred_element_type=F32)


def mask_rows(mask_ref, counts_ref):
    row = iota((ROWS, 64), 0)
    brick = (row >> 2) & 3
    held = mask_ref[...].astype(F32)
    spread = jnp.zeros((ROWS, 64), F32)
    for b in range(4):
        spread = jnp.where(brick == b, held[b : b + 1, :], spread)
    keep = (iota((ROWS, 64), 1) == (natural_of(row) & 63)) & (brick < counts_ref[0])
    return jnp.sum(jnp.where(keep, spread, 0.0), axis=1, keepdims=True)


def pickers(table_ref):
    row = iota((128, 27), 0) & 63
    shift, brick, k = row >> 4, (row >> 2) & 3, row & 3
    moved = k + shift - 1
    step = jnp.where(moved < 0, 0, jnp.where(moved > 3, 2, 1))
    held = table_ref[...].astype(F32)
    spread = jnp.zeros((128, 27), F32)
    for b in range(4):
        spread = jnp.where(brick == b, held[b : b + 1, :], spread)
    lane = iota((128, 128), 1)
    wide = iota((128, 128), 0) & 63
    source = ((wide & 3) + (wide >> 4) - 1) & 3
    fits = ((lane & 3) == source) & (wide < 48)
    picks = {}
    for qa in range(3):
        for qb in range(3):
            chosen = iota((128, 27), 1) == qa * 9 + qb * 3 + step
            entry = jnp.sum(jnp.where(chosen, spread, 0.0), axis=1, keepdims=True)
            hit = fits & (entry.astype(jnp.int32) == (lane >> 2)) & (lane < 48)
            picks[qa, qb] = hit.astype(F32)
    return picks


def places():
    for wi in range(6):
        for wj in range(6):
            qa, qb = (wi + 3) // 4, (wj + 3) // 4
            yield wi, wj, (qa, qb), (wi + 3) % 4, (wj + 3) % 4


def gather_windows(picks, lower, own, upper, win):
    half = {key: value[:48, :48].astype(BF16) for key, value in picks.items()}
    for wi, wj, q, i, j in places():
        at = pl.ds((i * 4 + j) * SIDE, SIDE)
        source = jnp.concatenate([lower[at], own[at], upper[at]], 0)
        got = mat(half[q], source).astype(BF16)
        for c in range(3):
            win[c, wi, wj] = got[c * SIDE : (c + 1) * SIDE]


def build_stack(win, stack):
    for o in range(27):
        a, b, c = o // 9, o // 3 % 3, o % 3
        stack[:, o * 256 : (o + 1) * 256] = win[c, a : a + 4, b : b + 4].reshape(ROWS, 256)


def spread_back(picks, grad, weight_ref, acc, own, lower, upper):
    acc[...] = jnp.zeros(acc.shape, F32)
    for o in range(27):
        a, b, c = o // 9, o // 3 % 3, o % 3
        part = lax.dot_general(
            grad,
            weight_ref[o * 256 : (o + 1) * 256, :],
            (((1,), (1,)), ((), ())),
            preferred_element_type=F32,
        )
        acc[c, a : a + 4, b : b + 4] += part.reshape(4, 4, SIDE, 256)
    turned = {key: value.T[:48].astype(BF16) for key, value in picks.items()}
    pad = jnp.zeros((SIDE, 256), BF16)
    totals = {}
    for wi, wj, q, i, j in places():
        held = acc[:, wi, wj].reshape(48, 256)
        high = held.astype(BF16)
        low = (held - high.astype(F32)).astype(BF16)
        got = mat(turned[q], jnp.concatenate([high, pad, low, pad], 0))
        totals[i, j] = totals[i, j] + got if (i, j) in totals else got
    for (i, j), value in totals.items():
        at = pl.ds((i * 4 + j) * SIDE, SIDE)
        lower[at] = value[:16].astype(BF16)
        own[at] = value[16:32]
        upper[at] = value[32:48].astype(BF16)


def first_kernel(feats, cot, mask, table, counts, w2, x0, g2, own, lower, upper, acc):
    keep = mask_rows(mask, counts)
    turn = to_rows()
    x0[...] = (mat(turn, feats[...]) * keep).astype(BF16)
    grad = (mat(turn, cot[...]) * keep).astype(BF16)
    g2[...] = grad
    spread_back(pickers(table), grad, w2, acc, own, lower, upper)


def second_kernel(
    x0_low, x0, x0_up, d_own, d_up, d_low, mask, table, counts, w1,
    a1, own, lower, upper, grad_w, win, stack, acc,
):
    keep = mask_rows(mask, counts)
    picks = pickers(table)
    gather_windows(picks, x0_low, x0, x0_up, win)
    build_stack(win, stack)
    y1 = mat(stack[...], w1[...]) * keep
    sig = 1.0 / (1.0 + jnp.exp(-y1))
    a1[...] = (y1 * sig).astype(BF16)
    da1 = d_own[...] + d_up[...].astype(F32) + d_low[...].astype(F32)
    g1 = (da1 * keep * (sig * (1.0 + y1 * (1.0 - sig)))).astype(BF16)
    for o in range(27):
        at = slice(o * 256, (o + 1) * 256)
        grad_w[at, :] = lax.dot_general(
            stack[:, at], g1, (((0,), (0,)), ((), ())), preferred_element_type=F32
        )
    spread_back(picks, g1, w1, acc, own, lower, upper)


def third_kernel(
    a_low, a1, a_up, f_own, f_up, f_low, x0, g2, mask, table, counts, w2,
    block_out, feats_grad, win, stack,
):
    keep = mask_rows(mask, counts)
    gather_windows(pickers(table), a_low, a1, a_up, win)
    build_stack(win, stack)
    y2 = mat(stack[...], w2[...]) * keep
    out = (y2 + x0[...].astype(F32)).astype(BF16)
    turn = from_rows()
    block_out[...] = mat(turn, out).astype(BF16)
    total = f_own[...] + f_up[...].astype(F32) + f_low[...].astype(F32)
    grad = (keep * (total + g2[...].astype(F32))).astype(BF16)
    feats_grad[...] = mat(turn, grad).astype(BF16)


def peer(z, y, core):
    return {"gx": z * 4 + y * 2 + core}


def remote(source, target, send_sem, recv_sem, device):
    return pltpu.make_async_remote_copy(
        src_ref=source, dst_ref=target, send_sem=send_sem, recv_sem=recv_sem,
        device_id=device, device_id_type=pl.DeviceIdType.MESH,
    )


def rows_of(kind):
    return jax.ShapeDtypeStruct((ROWS, 256), kind)


PARAMS = pltpu.CompilerParams(vmem_limit_bytes=50 * 2**20)
WIN = pltpu.VMEM((3, 6, 6, SIDE, 256), BF16)
ACC = pltpu.VMEM((3, 6, 6, SIDE, 256), F32)
STACK = pltpu.VMEM((ROWS, 6912), BF16)


def shifted(value, steps):
    count = lax.axis_size("gx")
    first, last = (max(0, -steps), min(count, count - steps))
    return lax.ppermute(value, "gx", [(source, source + steps) for source in range(first, last)])


def exchange(field, lower, upper):
    up = shifted(jnp.concatenate([field, upper], 0), 1)
    down = shifted(jnp.concatenate([field, lower], 0), -1)
    return up[:ROWS], down[:ROWS], up[ROWS:], down[ROWS:]


def whole_kernel(
    feats, cot, mask, table, counts, w1_hbm, w2_hbm,
    block_out, feats_grad, grad_out,
    w1, w2, win, stack, acc, g2, own, grad, field, from_low, from_up, down_sum, up_sum,
    sum_low, sum_up, to_core, from_core, to_y, from_y, held, to_z, from_z,
    load, ring_send, ring_recv, sum_send, sum_recv,
    core_send, core_recv, y_send, y_recv, z_send, z_recv,
):
    me, devices, share = lax.axis_index("gx"), lax.axis_size("gx"), grad_out.shape[0]
    z, y, core = me // 4, (me // 2) % 2, me % 2
    targets = [3 - z, (z + 2) % 4, z + 1 - 2 * (z % 2), z]
    partners = [peer(z, y, 1 - core), peer(z, 1 - y, core)]
    partners += [peer(target, y, core) for target in targets[:3]]
    other = {"gx": (me + 2 * core - 1 + devices) % devices}
    above, below = {"gx": (me + 1) % devices}, {"gx": (me - 1 + devices) % devices}
    barrier = pltpu.get_barrier_semaphore()
    for device in [*partners, other]:
        pl.semaphore_signal(barrier, inc=1, device_id=device, device_id_type=pl.DeviceIdType.MESH)
    load_w2 = pltpu.make_async_copy(w2_hbm, w2, load.at[0])
    load_w1 = pltpu.make_async_copy(w1_hbm, w1, load.at[1])
    load_w2.start()
    load_w1.start()
    has_above, has_below = me < devices - 1, me > 0

    @pl.when(me == 0)
    def _():
        from_low[...] = jnp.zeros(from_low.shape, BF16)
        sum_low[...] = jnp.zeros(sum_low.shape, BF16)

    @pl.when(me == devices - 1)
    def _():
        from_up[...] = jnp.zeros(from_up.shape, BF16)
        sum_up[...] = jnp.zeros(sum_up.shape, BF16)

    def ring(n, up_source, low_slot, down_source, up_slot, send, recv):
        return (
            remote(up_source.at[n], low_slot.at[n], send.at[n, 0], recv.at[n, 0], above),
            remote(down_source.at[n], up_slot.at[n], send.at[n, 1], recv.at[n, 1], below),
        )

    def start(pair):
        pl.when(has_above)(pair[0].start)
        pl.when(has_below)(pair[1].start)

    def wait_recv(pair):
        pl.when(has_below)(pair[0].wait_recv)
        pl.when(has_above)(pair[1].wait_recv)

    def wait_send(pair):
        pl.when(has_above)(pair[0].wait_send)
        pl.when(has_below)(pair[1].wait_send)

    fields = [ring(n, field, from_low, field, from_up, ring_send, ring_recv) for n in range(2)]
    sums = [ring(n, up_sum, sum_low, down_sum, sum_up, sum_send, sum_recv) for n in range(2)]

    keep = mask_rows(mask, counts)
    turn = to_rows()
    field[0] = (mat(turn, feats[...]) * keep).astype(BF16)
    pl.semaphore_wait(barrier, len(partners) + 1)
    start(fields[0])
    g2[...] = (mat(turn, cot[...]) * keep).astype(BF16)
    picks = pickers(table)
    load_w2.wait()
    spread_back(picks, g2[...], w2, acc, own, down_sum.at[0], up_sum.at[0])
    start(sums[0])
    load_w1.wait()
    wait_recv(fields[0])
    gather_windows(picks, from_low.at[0], field.at[0], from_up.at[0], win)
    build_stack(win, stack)
    y1 = mat(stack[...], w1[...]) * keep
    sig = 1.0 / (1.0 + jnp.exp(-y1))
    field[1] = (y1 * sig).astype(BF16)
    start(fields[1])
    wait_recv(sums[0])
    da1 = own[...] + sum_up[0].astype(F32) + sum_low[0].astype(F32)
    g1 = (da1 * keep * (sig * (1.0 + y1 * (1.0 - sig)))).astype(BF16)
    half = share // 32 * 16
    pieces = [(0, half), (half, share - half)]

    def part(target, side, lane, first, size):
        start_row = (target * 4 + side * 2 + lane) * share + first
        return grad[pl.ds(pl.multiple_of(start_row, 16), size), :]

    by_core, by_y, by_z = [], [], []

    def grad_to_core(step):
        target = targets[step]
        first = target * 27 // 4 - target // 3
        for n in range(8):
            at = pl.ds(pl.multiple_of((first + n) * 256, 256), 256)
            grad[at, :] = lax.dot_general(
                stack[:, at], g1, (((0,), (0,)), ((), ())), preferred_element_type=F32
            )
        for side in range(2):
            to_core[step, side] = part(target, side, 1 - core, 0, share).astype(BF16)
        copy = remote(
            to_core.at[step], from_core.at[step], core_send.at[step], core_recv.at[step],
            partners[0],
        )
        copy.start()
        by_core.append(copy)

    def core_to_y(step):
        by_core[step].wait_recv()
        target = targets[step]
        for n, (first, size) in enumerate(pieces):
            at = pl.ds(first, size)
            away = part(target, 1 - y, core, first, size)
            to_y[step, at] = (away + from_core[step, 1 - y, at].astype(F32)).astype(BF16)
            copy = remote(
                to_y.at[step, at], from_y.at[step, at], y_send.at[step, n], y_recv.at[step, n],
                partners[1],
            )
            copy.start()
            by_y.append(copy)
        held[step] = part(target, y, core, 0, share) + from_core[step, y].astype(F32)

    def y_to_z(step, n):
        by_y[2 * step + n].wait_recv()
        at = pl.ds(*pieces[n])
        to_z[step, at] = (held[step, at] + from_y[step, at].astype(F32)).astype(BF16)
        copy = remote(
            to_z.at[step, at], from_z.at[step, at], z_send.at[step, n], z_recv.at[step, n],
            partners[2 + step],
        )
        copy.start()
        by_z.append(copy)

    grad_to_core(0)
    grad_to_core(1)
    core_to_y(0)
    grad_to_core(2)
    core_to_y(1)
    grad_to_core(3)
    core_to_y(2)
    core_to_y(3)
    y_to_z(0, 0)
    spread_back(picks, g1, w1, acc, own, down_sum.at[1], up_sum.at[1])
    y_to_z(0, 1)
    start(sums[1])
    wait_recv(fields[1])
    gather_windows(picks, from_low.at[1], field.at[1], from_up.at[1], win)
    build_stack(win, stack)
    y_to_z(1, 0)
    y2 = mat(stack[...], w2[...]) * keep
    block_out[...] = (y2 + field[0].astype(F32)).astype(BF16)
    y_to_z(1, 1)
    y_to_z(2, 0)
    y_to_z(2, 1)
    wait_recv(sums[1])
    total = own[...] + sum_up[1].astype(F32) + sum_low[1].astype(F32)
    feats_grad[...] = (keep * (total + g2[...].astype(F32))).astype(BF16)
    by_y[6].wait_recv()
    by_y[7].wait_recv()
    grad_out[...] = held[3] + from_y[3].astype(F32)
    for step in range(3):
        by_z[2 * step].wait_recv()
        by_z[2 * step + 1].wait_recv()
        grad_out[...] += from_z[step].astype(F32)
    for copy in by_core + by_y + by_z:
        copy.wait_send()
    for pair in fields + sums:
        wait_send(pair)


def last_kernel(block_rows, grad_rows, share, block_out, feats_grad, grad_out):
    turn = from_rows()
    block_out[...] = mat(turn, block_rows[...]).astype(BF16)
    feats_grad[...] = mat(turn, grad_rows[...]).astype(BF16)
    grad_out[...] = share[...]


def in_one(feats, voxel_mask, brick_table, counts, weight_one, weight_two, cotangent):
    per, vb, ch = feats.shape
    share = (weight_one.shape[0] // lax.axis_size("gx"), ch)
    anywhere = pl.BlockSpec(memory_space=pl.ANY)
    pair = pltpu.VMEM((2, ROWS, ch), BF16)
    shapes = [rows_of(BF16), rows_of(BF16), jax.ShapeDtypeStruct(share, F32)]
    parts = pl.pallas_call(
        whole_kernel,
        out_shape=shapes,
        in_specs=[VMEM, VMEM, VMEM, VMEM, SMEM, anywhere, anywhere],
        out_specs=[VMEM] * 3,
        scratch_shapes=[
            pltpu.VMEM(weight_one.shape, BF16),
            pltpu.VMEM(weight_two.shape, BF16),
            WIN,
            STACK,
            ACC,
            pltpu.VMEM((ROWS, ch), BF16),
            pltpu.VMEM((ROWS, ch), F32),
            pltpu.VMEM(weight_one.shape, F32),
            *[pair] * 7,
            pltpu.VMEM((4, 2, *share), BF16),
            pltpu.VMEM((4, 2, *share), BF16),
            pltpu.VMEM((4, *share), BF16),
            pltpu.VMEM((4, *share), BF16),
            pltpu.VMEM((4, *share), F32),
            pltpu.VMEM((3, *share), BF16),
            pltpu.VMEM((3, *share), BF16),
            pltpu.SemaphoreType.DMA((2,)),
            *[pltpu.SemaphoreType.DMA((2, 2))] * 4,
            *[pltpu.SemaphoreType.DMA((4,))] * 2,
            *[pltpu.SemaphoreType.DMA((4, 2))] * 2,
            *[pltpu.SemaphoreType.DMA((3, 2))] * 2,
        ],
        compiler_params=pltpu.CompilerParams(
            vmem_limit_bytes=56 * 2**20, collective_id=0, has_side_effects=True
        ),
    )(
        feats.reshape(per * vb, ch), cotangent.reshape(per * vb, ch), voxel_mask, brick_table,
        counts, weight_one, weight_two,
    )
    block_out, feats_grad, grad_one = pl.pallas_call(
        last_kernel, out_shape=shapes, in_specs=[VMEM] * 3, out_specs=[VMEM] * 3,
        compiler_params=pltpu.CompilerParams(vmem_limit_bytes=60 * 2**20),
    )(*parts)
    return (block_out.reshape(per, vb, ch), feats_grad.reshape(per, vb, ch), grad_one)


def on_device(feats, voxel_mask, brick_table, counts, weight_one, weight_two, cotangent):
    if lax.axis_size("gx") == 16:
        return in_one(feats, voxel_mask, brick_table, counts, weight_one, weight_two, cotangent)
    per, vb, ch = feats.shape
    kc = weight_one.shape[0]
    small = (voxel_mask, brick_table, counts)
    small_specs = [VMEM, VMEM, SMEM]
    x0, g2, d_own, d_lower, d_upper = pl.pallas_call(
        first_kernel,
        out_shape=[rows_of(BF16), rows_of(BF16), rows_of(F32), rows_of(BF16), rows_of(BF16)],
        in_specs=[VMEM, VMEM, *small_specs, VMEM],
        out_specs=[VMEM] * 5,
        scratch_shapes=[ACC],
        compiler_params=PARAMS,
    )(feats.reshape(per * vb, ch), cotangent.reshape(per * vb, ch), *small, weight_two)
    x_low, x_up, d_low, d_up = exchange(x0, d_lower, d_upper)
    a1, f_own, f_lower, f_upper, grad_w = pl.pallas_call(
        second_kernel,
        out_shape=[
            rows_of(BF16), rows_of(F32), rows_of(BF16), rows_of(BF16),
            jax.ShapeDtypeStruct((kc, ch), F32),
        ],
        in_specs=[VMEM] * 6 + small_specs + [VMEM],
        out_specs=[VMEM] * 5,
        scratch_shapes=[WIN, STACK, ACC],
        compiler_params=PARAMS,
    )(x_low, x0, x_up, d_own, d_up, d_low, *small, weight_one)
    grad_one = lax.psum_scatter(grad_w, "gx", scatter_dimension=0, tiled=True)
    a_low, a_up, f_low, f_up = exchange(a1, f_lower, f_upper)
    block_out, feats_grad = pl.pallas_call(
        third_kernel,
        out_shape=[rows_of(BF16), rows_of(BF16)],
        in_specs=[VMEM] * 8 + small_specs + [VMEM],
        out_specs=[VMEM] * 2,
        scratch_shapes=[WIN, STACK],
        compiler_params=PARAMS,
    )(a_low, a1, a_up, f_own, f_up, f_low, x0, g2, *small, weight_two)
    return (block_out.reshape(per, vb, ch), feats_grad.reshape(per, vb, ch), grad_one)


def solution(mesh):
    split = ("scene", "gx")
    in_specs = (
        P(split, None, None), P(split, None), P(split, None), P(split), P(), P(),
        P(split, None, None),
    )
    out_specs = (P(split, None, None), P(split, None, None), P(split, None))
    return jax.shard_map(
        on_device, mesh=mesh, in_specs=in_specs, out_specs=out_specs, check_vma=False
    )
```
